128 devices in a mesh: ctx: 32 (over y, x, core), head: 4 (over z).
Axes of the slice: x: 4, y: 4, z: 4, core: 2. Of those that a mesh axis runs over, the one named last changes fastest.
Arguments:
- queries: bfloat16 [16384, 4096], P('ctx', 'head'), may hold values from -5 to 5
- keys: bfloat16 [16384, 512], P('ctx', 'head'), may hold values from -5 to 5
- values: bfloat16 [16384, 512], P('ctx', 'head'), may hold values from -6 to 6
- doc_ids: int32 [16384], replicated, may hold values from 0 to 31, never falling along the last dimension, each value on 1 to 1536 neighbouring positions
- out_weight: bfloat16 [4096, 8192], P(None, 'head'), may hold values from -0.09375 to 0.09375
Outputs:
- layer_out: bfloat16 [16384, 8192], P('ctx', 'head')
The draws below stay inside these ranges and needn't reach their ends.
Inputs may be any that keep to these rules, and one draw needn't show every extreme that they name: `doc_ids`: every document holds at most 1536 tokens, and one holds exactly that many.
All inputs are finite; a program needn't handle non-finite values.
Results may differ from the reference program's by a relative error of at most 0.0053.
Values may be sent and summed in bfloat16 or wider, within the bound.
No kernel may reach another device: no remote copies, remote signals or barrier semaphores. Data moves between devices by JAX's collectives and lax.ppermute only.
A program may use at most 128 MiB of HBM per device.

```python
import math
import jax
import jax.numpy as jnp
import numpy as np
from jax import lax

D = 8192
QUERY_HEAD_COUNT = 32
KEY_VALUE_HEADS = 4
HEAD_SIZE = 128
TOKENS_PER_SLICE = 512
REACH = 3
PACK_TOKENS = 16384
DOCS = 32


def draw_queries(key, part):
    sampled_values = jnp.clip(jax.random.normal(jax.random.fold_in(key, 1), (PACK_TOKENS, QUERY_HEAD_COUNT, HEAD_SIZE), jnp.float32), -4.5, 4.5)
    return sampled_values.reshape(PACK_TOKENS, QUERY_HEAD_COUNT * HEAD_SIZE).astype(jnp.bfloat16)


def draw_keys(key, part):
    sampled_values = jnp.clip(jax.random.normal(jax.random.fold_in(key, 2), (PACK_TOKENS, KEY_VALUE_HEADS, HEAD_SIZE), jnp.float32), -4.5, 4.5)
    return sampled_values.reshape(PACK_TOKENS, KEY_VALUE_HEADS * HEAD_SIZE).astype(jnp.bfloat16)


def steps_of(key, dims, cuts, smallest, top_value):
    factor_of = 1.0
    for axis_at, shards_of in cuts:
        steps = jax.random.uniform(jax.random.fold_in(jax.random.fold_in(key, 6), axis_at), (shards_of,), jnp.float32, smallest / len(cuts), top_value / len(cuts))
        factor_of = factor_of * jnp.repeat(jnp.exp(steps), dims[axis_at] // shards_of).reshape((-1,) + (1,) * (len(dims) - 1 - axis_at))
    return factor_of


def split_up(amount, total, bound, slope):
    weights = [(1 << 20) // math.isqrt(standing ** slope) + 1 for standing in range(2, amount + 1)]
    spare, given = total - bound - (amount - 1), [1] * (amount - 1)
    while spare > 0:
        movable = [i for i in range(amount - 1) if given[i] < bound]
        whole, left = sum([weights[i] for i in movable]), spare
        for i in movable:
            extra = min(bound - given[i], max(1, left * weights[i] // whole), spare)
            given[i] = given[i] + extra
            spare = spare - extra
    return np.array([bound] + given)


def uneven_parts(own_key, number_of, total, bound, slope):
    if number_of == 2:
        one = jax.random.randint(own_key, (), max(1, total - bound), min(bound, total - 1) + 1)
        return jnp.stack([one, total - one])
    sizes = jnp.asarray(split_up(number_of, total, bound, slope), jnp.int32)
    twos = (number_of - 1) // 2
    giver, taker = sizes[1:1 + 2 * twos:2], sizes[2:2 + 2 * twos:2]
    margin = jnp.minimum(giver - 1, bound - taker)
    moved = jax.random.randint(jax.random.fold_in(own_key, 1), (twos,), 0, 1 << 20) % (margin + 1)
    sizes = sizes.at[1:1 + 2 * twos:2].set(giver - moved).at[2:2 + 2 * twos:2].set(taker + moved)
    return sizes[jax.random.permutation(jax.random.fold_in(own_key, 2), number_of)]


def bell_draw(own_key, dims, deviation, reach, shards=(), held_as=jnp.bfloat16):
    loudness = steps_of(own_key, dims, shards, -0.22, 0.18) if shards else 1.0
    values = jax.random.normal(own_key, dims, jnp.float32) * deviation * loudness
    return jnp.minimum(jnp.maximum(values, -reach), reach).astype(held_as)


def setup_inputs(seed: int = 0) -> dict:
    arg_keys = jax.random.split(jax.random.key(seed), 6)
    queries = draw_queries(jax.random.fold_in(arg_keys[5], 71), 0)
    keys = draw_keys(jax.random.fold_in(arg_keys[5], 71), 0)
    values = bell_draw(arg_keys[2], (PACK_TOKENS, KEY_VALUE_HEADS * HEAD_SIZE), 1.0, 6.0, ((0, 32), (1, 4)))
    doc_ids = jnp.searchsorted(jnp.cumsum(uneven_parts(arg_keys[3], DOCS, PACK_TOKENS, REACH * TOKENS_PER_SLICE, 2)), jnp.arange(PACK_TOKENS), side="right").astype(jnp.int32)
    out_weight = bell_draw(arg_keys[4], (QUERY_HEAD_COUNT * HEAD_SIZE, D), (QUERY_HEAD_COUNT * HEAD_SIZE) ** -0.5, 0.09375, ((1, 4),))
    return dict(queries=queries, keys=keys, values=values, doc_ids=doc_ids, out_weight=out_weight)


def reference(queries, keys, values, doc_ids, out_weight):
    group_width = QUERY_HEAD_COUNT // KEY_VALUE_HEADS
    local_span = (REACH + 1) * TOKENS_PER_SLICE
    leading_rows = REACH * TOKENS_PER_SLICE
    key_padding = jnp.concatenate([jnp.zeros((leading_rows, KEY_VALUE_HEADS * HEAD_SIZE), keys.dtype), keys], 0)
    value_padding = jnp.concatenate([jnp.zeros((leading_rows, KEY_VALUE_HEADS * HEAD_SIZE), values.dtype), values], 0)
    doc_pad = jnp.concatenate([jnp.full((leading_rows,), -1, jnp.int32), doc_ids.astype(jnp.int32)], 0)
    key_rel = jnp.arange(local_span, dtype=jnp.int32)
    query_rel = leading_rows + jnp.arange(TOKENS_PER_SLICE, dtype=jnp.int32)

    def one_block(block_index):
        start_row = (block_index * TOKENS_PER_SLICE).astype(jnp.int32)
        query_row_block = lax.dynamic_slice_in_dim(queries, start_row, TOKENS_PER_SLICE, 0).astype(jnp.float32)
        query_row_block = query_row_block.reshape(TOKENS_PER_SLICE, KEY_VALUE_HEADS, group_width, HEAD_SIZE)
        key_row_block = lax.dynamic_slice_in_dim(key_padding, start_row, local_span, 0).astype(jnp.float32).reshape(local_span, KEY_VALUE_HEADS, HEAD_SIZE)
        value_row_block = lax.dynamic_slice_in_dim(value_padding, start_row, local_span, 0).astype(jnp.float32).reshape(local_span, KEY_VALUE_HEADS, HEAD_SIZE)
        key_docs = lax.dynamic_slice_in_dim(doc_pad, start_row, local_span, 0)
        query_docs = lax.dynamic_slice_in_dim(doc_ids.astype(jnp.int32), start_row, TOKENS_PER_SLICE, 0)
        visible = (query_docs[:, None] == key_docs[None, :]) & (key_rel[None, :] <= query_rel[:, None])
        scores = jnp.einsum("qgjd,kgd->gjqk", query_row_block, key_row_block) * (HEAD_SIZE ** -0.5)
        masked = jnp.where(visible, scores, -jnp.inf)
        row_peak = jnp.max(masked, axis=3, keepdims=True)
        exponent = jnp.where(visible, jnp.exp(scores - row_peak), 0.0)
        row_total = jnp.sum(exponent, axis=3, keepdims=True)
        weights = lax.optimization_barrier(exponent.astype(jnp.bfloat16)).astype(jnp.float32)
        mixture = jnp.einsum("gjqk,kgd->gjqd", weights, value_row_block) / row_total
        return jnp.transpose(mixture, (2, 0, 1, 3)).reshape(TOKENS_PER_SLICE, QUERY_HEAD_COUNT * HEAD_SIZE).astype(jnp.bfloat16)

    attended = lax.map(one_block, jnp.arange(PACK_TOKENS // TOKENS_PER_SLICE, dtype=jnp.int32))
    attended = attended.reshape(PACK_TOKENS, QUERY_HEAD_COUNT * HEAD_SIZE)
    return jnp.dot(attended, out_weight, preferred_element_type=jnp.float32).astype(jnp.bfloat16)
```

```python
import functools
import math

import jax
import jax.numpy as jnp
from jax import lax
from jax.experimental import pallas as pl
from jax.experimental.pallas import tpu as pltpu
from jax.sharding import PartitionSpec as P

HEAD_SIZE = 128
REACH = 3
EXPONENT_SCALE = math.log2(math.e) * HEAD_SIZE ** (-0.5)
HIDDEN = -1e30
CONTRACT_LAST = (((1,), (1,)), ((), ()))
PLAIN = (((1,), (0,)), ((), ()))
VMEM = pl.BlockSpec(memory_space=pltpu.VMEM)
SMEM = pl.BlockSpec(memory_space=pltpu.SMEM)


def beside_ones(values):
    return jnp.concatenate([values, jnp.ones_like(values)], 1)


def wide(column, count):
    return column if count == 1 else jnp.concatenate([column] * count, 1)


def block_update(q, keys, values, bias, before, mixed):
    span = keys.shape[0]
    s = lax.dot_general(q, keys, CONTRACT_LAST, preferred_element_type=jnp.float32)
    if bias is not None:
        s = s + bias
    peak = jnp.broadcast_to(jnp.max(s, axis=1, keepdims=True), (q.shape[0], HEAD_SIZE))
    if before is not None:
        peak = jnp.maximum(before, peak)
    weights = jnp.exp2((s - wide(peak, span // HEAD_SIZE)) * EXPONENT_SCALE).astype(jnp.bfloat16)
    mix = lax.dot_general(weights, beside_ones(values), PLAIN, preferred_element_type=jnp.float32)
    if before is not None:
        mix = mix + mixed * wide(jnp.exp2((before - peak) * EXPONENT_SCALE), 2)
    return peak, mix


def own_kernel(q_ref, own_ref, qdoc_ref, kdoc_ref, peak_ref, mix_ref, bias_ref):
    rows = q_ref.shape[0]
    half = rows // 2
    heads = q_ref.shape[1] // HEAD_SIZE
    own_at = REACH * rows
    for part in range(2):
        span = (part + 1) * half
        at = part * half
        row = at + lax.broadcasted_iota(jnp.int32, (half, span), 0)
        col = lax.broadcasted_iota(jnp.int32, (half, span), 1)
        doc = wide(qdoc_ref[at:at + half, :], span // HEAD_SIZE)
        seen = (doc == kdoc_ref[0:1, own_at:own_at + span]) & (col <= row)
        bias_ref[:, 0:span] = jnp.where(seen, 0.0, HIDDEN)
        for head in range(heads):
            q = q_ref[at:at + half, head * HEAD_SIZE:(head + 1) * HEAD_SIZE]
            peak, mix = block_update(q, own_ref[0:span, :], own_ref[rows:rows + span, :], bias_ref[:, 0:span], None, None)
            peak_ref[head, at:at + half, :] = peak
            mix_ref[head, at:at + half, :] = mix


def rest_kernel(first_head, heads, edge_ref, q_ref, peak_ref, mix_ref, k1_ref, k2_ref, k3_ref, qdoc_ref, kdoc_ref,
                out_ref, peak_now, mix_now, bias_ref):
    rows = q_ref.shape[0]
    half = rows // 2
    peak_now[...] = peak_ref[first_head:first_head + heads]
    mix_now[...] = mix_ref[first_head:first_head + heads]

    def update(part, ref, at, span, window_at, masked):
        here = slice(part * half, (part + 1) * half)
        if masked:
            doc = wide(qdoc_ref[here, :], span // HEAD_SIZE)
            bias_ref[:, 0:span] = jnp.where(doc == kdoc_ref[0:1, window_at:window_at + span], 0.0, HIDDEN)
        for head in range(heads):
            column = (first_head + head) * HEAD_SIZE
            peak, mix = block_update(
                q_ref[here, column:column + HEAD_SIZE], ref[at:at + span, :], ref[rows + at:rows + at + span, :],
                bias_ref[:, 0:span] if masked else None, peak_now[head, here, :], mix_now[head, here, :])
            peak_now[head, here, :] = peak
            mix_now[head, here, :] = mix

    for part in range(2):
        first_doc = edge_ref[2 * (2 * REACH + part)]
        last_doc = edge_ref[2 * (2 * REACH + part) + 1]
        for ref, shard, pieces in ((k1_ref, 2, ((0, rows),)), (k2_ref, 1, ((0, rows),)), (k3_ref, 0, ((half, half), (0, half)))):
            for at, span in pieces:
                lo = edge_ref[2 * (2 * shard + at // half)]
                hi = edge_ref[2 * (2 * shard + (at + span) // half - 1) + 1]
                window_at = shard * rows + at

                @pl.when((hi == first_doc) & (lo == last_doc))
                def _():
                    update(part, ref, at, span, window_at, False)

                @pl.when((hi == first_doc) & (lo != last_doc))
                def _():
                    update(part, ref, at, span, window_at, True)

    for head in range(heads):
        mix = mix_now[head, :, 0:HEAD_SIZE] / mix_now[head, :, HEAD_SIZE:]
        out_ref[:, head * HEAD_SIZE:(head + 1) * HEAD_SIZE] = mix.astype(jnp.bfloat16)


def attend_own(queries, own, qdoc, kdoc):
    rows, width = queries.shape
    heads = width // HEAD_SIZE
    return pl.pallas_call(
        own_kernel,
        in_specs=[VMEM] * 4,
        out_specs=[VMEM] * 2,
        scratch_shapes=[pltpu.VMEM((rows // 2, rows), jnp.float32)],
        out_shape=[
            jax.ShapeDtypeStruct((heads, rows, HEAD_SIZE), jnp.float32),
            jax.ShapeDtypeStruct((heads, rows, 2 * HEAD_SIZE), jnp.float32),
        ],
        compiler_params=pltpu.CompilerParams(vmem_limit_bytes=8 * 2**20),
        cost_estimate=pl.CostEstimate(flops=2**32, bytes_accessed=2**20, transcendentals=2**20),
        name="attend_own",
    )(queries, own, qdoc, kdoc)


def attend_rest(queries, state, parts, qdoc, kdoc, edges, first_head, heads):
    rows = queries.shape[0]
    return pl.pallas_call(
        functools.partial(rest_kernel, first_head, heads),
        in_specs=[SMEM] + [VMEM] * 8,
        out_specs=VMEM,
        scratch_shapes=[
            pltpu.VMEM((heads, rows, HEAD_SIZE), jnp.float32),
            pltpu.VMEM((heads, rows, 2 * HEAD_SIZE), jnp.float32),
            pltpu.VMEM((rows // 2, rows), jnp.float32),
        ],
        out_shape=jax.ShapeDtypeStruct((rows, heads * HEAD_SIZE), jnp.bfloat16),
        compiler_params=pltpu.CompilerParams(vmem_limit_bytes=10 * 2**20),
        cost_estimate=pl.CostEstimate(flops=2**32, bytes_accessed=2**20, transcendentals=2**20),
        name=f"attend_rest_{first_head}",
    )(edges, queries, *state, *parts, qdoc, kdoc)


def project_kernel(counts, carried, at_ref, *refs):
    weight_refs, out_ref = refs[-1 - len(counts):-1], refs[-1]
    total = refs[sum(counts)][...] if carried else None
    n = 0
    for count, weight_ref in zip(counts, weight_refs):
        pieces = [refs[n + j][...] for j in range(count)]
        n += count
        left = pieces[0] if count == 1 else jnp.concatenate(pieces, 1)
        term = lax.dot_general(left, weight_ref[...], PLAIN, preferred_element_type=jnp.float32)
        total = term if total is None else total + term
    out_ref[...] = total.astype(out_ref.dtype)


def project(terms, at, weight, carried, out_dtype, name, columns=512, vmem=48):
    rows = terms[0][0].shape[0]
    width = weight.shape[1]
    depth = sum(piece.shape[1] for piece in terms[0])
    pieces = [piece for term in terms for piece in term]
    tile = pl.BlockSpec((rows, columns), lambda n, at: (0, n))
    weights = [pl.BlockSpec((depth, columns), lambda n, at, i=i: (at[i], n)) for i in range(len(terms))]
    return pl.pallas_call(
        functools.partial(project_kernel, tuple(len(t) for t in terms), carried is not None),
        grid_spec=pltpu.PrefetchScalarGridSpec(
            num_scalar_prefetch=1,
            grid=(width // columns,),
            in_specs=[VMEM] * len(pieces) + ([tile] if carried is not None else []) + weights,
            out_specs=tile,
        ),
        out_shape=jax.ShapeDtypeStruct((rows, width), out_dtype),
        compiler_params=pltpu.CompilerParams(vmem_limit_bytes=vmem * 2**20),
        cost_estimate=pl.CostEstimate(flops=2**20, bytes_accessed=2**10, transcendentals=0),
        name=name,
    )(jnp.stack(at).astype(jnp.int32), *pieces, *([carried] if carried is not None else []), *[weight] * len(terms))


def once_here(value, *others):
    anywhere = pl.BlockSpec(memory_space=pl.ANY)
    return pl.pallas_call(
        lambda *refs: None,
        in_specs=[anywhere] * (1 + len(others)),
        out_specs=anywhere,
        out_shape=jax.ShapeDtypeStruct(value.shape, value.dtype),
        input_output_aliases={0: 0},
        compiler_params=pltpu.CompilerParams(vmem_limit_bytes=2**20),
        cost_estimate=pl.CostEstimate(flops=0, bytes_accessed=0, transcendentals=0),
        name="once_here",
    )(value, *others)


def shards(queries, keys, values, doc_ids, out_weight):
    rows = keys.shape[0]
    shard = lax.axis_index("ctx")
    place = lax.axis_index("head")
    shard_count = lax.axis_size("ctx")
    places = lax.axis_size("head")
    other_core = [(i, i ^ 1) for i in range(shard_count)]

    def along_ctx(block, pairs):
        return lax.ppermute(block, "ctx", pairs)

    def along_head(block, step):
        return lax.ppermute(block, "head", [(i, (i + step) % places) for i in range(places)])

    own = jnp.concatenate([keys, values], 0)
    two_behind = along_ctx(own, [(i, i + 2) for i in range(shard_count - 2)])
    three_behind = along_ctx(own, [(i, i + 3) for i in range(1, shard_count - 3, 2)])
    beside = along_ctx(own, other_core)
    window = (REACH + 1) * rows
    padded = jnp.concatenate([jnp.full((REACH * rows,), -1, jnp.int32), doc_ids], 0)
    kdoc = lax.dynamic_slice_in_dim(padded, shard * rows, window, 0)
    half = rows // 2
    edges = jnp.stack([kdoc[::half], kdoc[half - 1::half]], 1).reshape(-1)
    qdoc = jnp.broadcast_to(kdoc[REACH * rows:, None], (rows, HEAD_SIZE))
    kdoc = kdoc[None, :]

    state = attend_own(queries, own, qdoc, kdoc)
    beside_two = along_ctx(two_behind, other_core)
    is_second = (shard % 2) == 1
    part1 = jnp.where(is_second, beside, beside_two)
    part2 = two_behind
    part3 = jnp.where(is_second, beside_two, three_behind)

    parts = (part1, part2, part3)
    split = 5
    a = attend_rest(queries, state, parts, qdoc, kdoc, edges, 0, split)
    a_up = along_head(a, 1)
    a_down = along_head(a, -1)
    b = attend_rest(queries, state, parts, qdoc, kdoc, edges, split, 8 - split)
    b_up = along_head(b, 1)
    b_down = along_head(b, -1)
    below = (place + places - 1) % places
    above = (place + 1) % places
    far = (place + 2) % places
    a_far = along_head(a_up, 1)
    b_down = once_here(b_down, a_down, b_up)
    b_far = along_head(b_down, -1)
    total = project([(a, b), (a_up, b_up), (a_down, b_down)], [place, below, above], out_weight, None, jnp.float32, "project_near")
    return project([(a_far, b_far)], [far], out_weight, total, jnp.bfloat16, "project_far", vmem=56)


def solution(mesh):
    in_specs = (P("ctx", "head"), P("ctx", "head"), P("ctx", "head"), P(), P(None, "head"))
    out_specs = P("ctx", "head")
    return jax.shard_map(shards, mesh=mesh, in_specs=in_specs, out_specs=out_specs, check_vma=False)
```

```python
import functools
import math

import jax
import jax.numpy as jnp
from jax import lax
from jax.experimental import pallas as pl
from jax.experimental.pallas import tpu as pltpu
from jax.sharding import PartitionSpec as P

HEAD_SIZE = 128
REACH = 3
EXPONENT_SCALE = math.log2(math.e) * HEAD_SIZE ** (-0.5)
HIDDEN = -1e30
CONTRACT_LAST = (((1,), (1,)), ((), ()))
PLAIN = (((1,), (0,)), ((), ()))
VMEM = pl.BlockSpec(memory_space=pltpu.VMEM)
SMEM = pl.BlockSpec(memory_space=pltpu.SMEM)


def beside_ones(values):
    return jnp.concatenate([values, jnp.ones_like(values)], 1)


def wide(column, count):
    return column if count == 1 else jnp.concatenate([column] * count, 1)


def block_update(q, keys, values, bias, before, mixed):
    span = keys.shape[0]
    s = lax.dot_general(q, keys, CONTRACT_LAST, preferred_element_type=jnp.float32)
    if bias is not None:
        s = s + bias
    peak = jnp.broadcast_to(jnp.max(s, axis=1, keepdims=True), (q.shape[0], HEAD_SIZE))
    if before is not None:
        peak = jnp.maximum(before, peak)
    weights = jnp.exp2((s - wide(peak, span // HEAD_SIZE)) * EXPONENT_SCALE).astype(jnp.bfloat16)
    mix = lax.dot_general(weights, beside_ones(values), PLAIN, preferred_element_type=jnp.float32)
    if before is not None:
        mix = mix + mixed * wide(jnp.exp2((before - peak) * EXPONENT_SCALE), 2)
    return peak, mix


def own_kernel(splits, q_ref, own_ref, kdoc_ref, *refs):
    *states, qdoc_ref, again_ref, bias_ref = refs
    again_ref[...] = own_ref[...]
    rows = q_ref.shape[0]
    half = rows // 2
    heads = q_ref.shape[1] // HEAD_SIZE
    own_at = REACH * rows
    qdoc_ref[...] = jnp.broadcast_to(kdoc_ref[0:1, own_at:own_at + rows], (HEAD_SIZE, rows)).T
    for part in range(2):
        span = (part + 1) * half
        at = part * half
        row = at + lax.broadcasted_iota(jnp.int32, (half, span), 0)
        col = lax.broadcasted_iota(jnp.int32, (half, span), 1)
        doc = wide(qdoc_ref[at:at + half, :], span // HEAD_SIZE)
        seen = (doc == kdoc_ref[0:1, own_at:own_at + span]) & (col <= row)
        bias_ref[:, 0:span] = jnp.where(seen, 0.0, HIDDEN)
        for head in range(heads):
            q = q_ref[at:at + half, head * HEAD_SIZE:(head + 1) * HEAD_SIZE]
            peak, mix = block_update(q, own_ref[0:span, :], own_ref[rows:rows + span, :], bias_ref[:, 0:span], None, None)
            group = sum(head >= first for first in splits) - 1
            states[2 * group][head - splits[group], at:at + half, :] = peak
            states[2 * group + 1][head - splits[group], at:at + half, :] = mix


def update_seen(docs_ref, q_ref, qdoc_ref, kdoc_ref, bias_ref, blocks, states):
    rows = q_ref.shape[0]
    half = rows // 2

    def update(part, ref, at, span, window_at, masked):
        here = slice(part * half, (part + 1) * half)
        if masked:
            doc = wide(qdoc_ref[here, :], span // HEAD_SIZE)
            bias_ref[:, 0:span] = jnp.where(doc == kdoc_ref[0:1, window_at:window_at + span], 0.0, HIDDEN)
        for first_head, peak_ref, mix_ref in states:
            for head in range(peak_ref.shape[0]):
                column = (first_head + head) * HEAD_SIZE
                peak, mix = block_update(
                    q_ref[here, column:column + HEAD_SIZE], ref[at:at + span, :], ref[rows + at:rows + at + span, :],
                    bias_ref[:, 0:span] if masked else None, peak_ref[head, here, :], mix_ref[head, here, :])
                peak_ref[head, here, :] = peak
                mix_ref[head, here, :] = mix

    own_at = REACH * rows
    for part in range(2):
        first_doc = docs_ref[own_at + part * half]
        last_doc = docs_ref[own_at + (part + 1) * half - 1]
        for ref, shard, pieces in blocks:
            for at, span in pieces:
                window_at = shard * rows + at
                lo, hi = docs_ref[window_at], docs_ref[window_at + span - 1]

                @pl.when((hi == first_doc) & (lo == last_doc))
                def _():
                    update(part, ref, at, span, window_at, False)

                @pl.when((hi == first_doc) & (lo != last_doc))
                def _():
                    update(part, ref, at, span, window_at, True)


def two_behind_kernel(docs_ref, q_ref, k2_ref, qdoc_ref, kdoc_ref, _, __, peak_ref, mix_ref, bias_ref):
    blocks = ((k2_ref, 1, ((0, q_ref.shape[0]),)),)
    update_seen(docs_ref, q_ref, qdoc_ref, kdoc_ref, bias_ref, blocks, ((0, peak_ref, mix_ref),))


def rest_kernel(first_head, heads, fetches, all_blocks, docs_ref, q_ref, beside_ref, k2_ref, beside_two_ref, three_ref,
                qdoc_ref, kdoc_ref, *refs):
    if fetches:
        weight_ref, _, _, peak_ref, mix_ref, out_ref, held_ref, bias_ref, k1_ref, k3_ref, fetched = refs
        fetch = pltpu.make_async_copy(weight_ref, held_ref, fetched)
        fetch.start()
    else:
        _, _, peak_ref, mix_ref, out_ref, bias_ref, k1_ref, k3_ref = refs
    rows = q_ref.shape[0]
    half = rows // 2
    second_core = lax.rem(lax.axis_index("ctx"), 2) == 1

    @pl.when(second_core)
    def _():
        k1_ref[...] = beside_ref[...]
        k3_ref[...] = beside_two_ref[...]

    @pl.when(jnp.logical_not(second_core))
    def _():
        k1_ref[...] = beside_two_ref[...]
        k3_ref[...] = three_ref[...]

    blocks = ((k1_ref, 2, ((0, rows),)), (k3_ref, 0, ((half, half), (0, half))))
    if all_blocks:
        blocks += ((k2_ref, 1, ((0, rows),)),)
    update_seen(docs_ref, q_ref, qdoc_ref, kdoc_ref, bias_ref, blocks, ((first_head, peak_ref, mix_ref),))
    for head in range(heads):
        mix = mix_ref[head, :, 0:HEAD_SIZE] / mix_ref[head, :, HEAD_SIZE:]
        out_ref[:, head * HEAD_SIZE:(head + 1) * HEAD_SIZE] = mix.astype(jnp.bfloat16)
    if fetches:
        fetch.wait()


def state_shapes(heads, rows):
    return [
        jax.ShapeDtypeStruct((heads, rows, HEAD_SIZE), jnp.float32),
        jax.ShapeDtypeStruct((heads, rows, 2 * HEAD_SIZE), jnp.float32),
    ]


ATTEND_COST = pl.CostEstimate(flops=2**32, bytes_accessed=2**20, transcendentals=2**20)


def attend_own(queries, own, kdoc, splits):
    rows, width = queries.shape
    ends = splits[1:] + (width // HEAD_SIZE,)
    return pl.pallas_call(
        functools.partial(own_kernel, splits),
        in_specs=[VMEM] * 3,
        out_specs=[VMEM] * (2 * len(splits) + 2),
        scratch_shapes=[pltpu.VMEM((rows // 2, rows), jnp.float32)],
        out_shape=[shape for first, end in zip(splits, ends) for shape in state_shapes(end - first, rows)]
        + [jax.ShapeDtypeStruct((rows, HEAD_SIZE), jnp.int32), jax.ShapeDtypeStruct(own.shape, own.dtype)],
        compiler_params=pltpu.CompilerParams(vmem_limit_bytes=8 * 2**20),
        cost_estimate=ATTEND_COST,
        name="attend_own",
    )(queries, own, kdoc)


def attend_two_behind(queries, block, qdoc, kdoc, state):
    rows = queries.shape[0]
    return pl.pallas_call(
        two_behind_kernel,
        in_specs=[SMEM] + [VMEM] * 6,
        out_specs=[VMEM] * 2,
        scratch_shapes=[pltpu.VMEM((rows // 2, rows), jnp.float32)],
        out_shape=state_shapes(state[0].shape[0], rows),
        input_output_aliases={5: 0, 6: 1},
        compiler_params=pltpu.CompilerParams(vmem_limit_bytes=8 * 2**20),
        cost_estimate=ATTEND_COST,
        name="attend_two_behind",
    )(kdoc.reshape(-1), queries, block, qdoc, kdoc, *state)


def attend_rest(queries, parts, qdoc, kdoc, state, first_head, all_blocks, weight=None):
    rows = queries.shape[0]
    heads = state[0].shape[0]
    fetches = weight is not None
    attended = jax.ShapeDtypeStruct((rows, heads * HEAD_SIZE), jnp.bfloat16)
    return pl.pallas_call(
        functools.partial(rest_kernel, first_head, heads, fetches, all_blocks),
        in_specs=[SMEM] + [VMEM] * 7 + [pl.BlockSpec(memory_space=pl.ANY)] * fetches + [VMEM] * 2,
        out_specs=[VMEM] * (3 + fetches),
        scratch_shapes=[
            pltpu.VMEM((rows // 2, rows), jnp.float32),
            pltpu.VMEM(parts[0].shape, jnp.bfloat16),
            pltpu.VMEM(parts[0].shape, jnp.bfloat16),
        ] + [pltpu.SemaphoreType.DMA] * fetches,
        out_shape=state_shapes(heads, rows) + [attended]
        + ([jax.ShapeDtypeStruct(weight.shape, weight.dtype)] if fetches else []),
        input_output_aliases={8 + fetches: 0, 9 + fetches: 1},
        compiler_params=pltpu.CompilerParams(vmem_limit_bytes=(24 if fetches else 8) * 2**20),
        cost_estimate=ATTEND_COST,
        name=f"attend_rest_{first_head}",
    )(kdoc.reshape(-1), queries, *parts, qdoc, kdoc, *[weight] * fetches, *state)[2:]


def project_kernel(count, carried, last, columns, starts, *refs):
    weight_ref, out_ref = refs[count], refs[count + 1 + carried]
    places = lax.axis_size("head")
    share = weight_ref.shape[0] // places
    copies = []
    for step in range(weight_ref.shape[1] // columns):
        here = slice(step * columns, (step + 1) * columns)
        total = refs[count + 1][:, here] if carried else None
        for i in range(count):
            hops, first_row = starts[i]
            place = lax.rem(lax.axis_index("head") + hops, places)
            rows = pl.ds(pl.multiple_of(place * share + first_row, HEAD_SIZE), refs[i].shape[1])
            term = lax.dot_general(refs[i][...], weight_ref[rows, here], PLAIN, preferred_element_type=jnp.float32)
            total = term if total is None else total + term
        if last:
            tile_ref, sems = refs[-2], refs[-1]
            tile_ref[step] = total.astype(out_ref.dtype)
            copies.append(pltpu.make_async_copy(tile_ref.at[step], out_ref.at[:, here], sems.at[step]))
            copies[-1].start()
        else:
            out_ref[:, here] = total
    for copy in copies:
        copy.wait()


def project(pieces, starts, weight, total, name, last=False, columns=512, flops=2**20):
    rows, width = pieces[0].shape[0], weight.shape[1]
    carried = total is not None
    args = [*pieces, weight] + [total] * carried
    tiles = width // columns
    if last:
        rest = dict(
            out_specs=pl.BlockSpec(memory_space=pl.ANY),
            scratch_shapes=[pltpu.VMEM((tiles, rows, columns), jnp.bfloat16), pltpu.SemaphoreType.DMA((tiles,))],
        )
    else:
        rest = dict(out_specs=VMEM, input_output_aliases={len(args) - 1: 0} if carried else {})
    return pl.pallas_call(
        functools.partial(project_kernel, len(pieces), carried, last, columns, starts),
        in_specs=[VMEM] * len(args),
        out_shape=jax.ShapeDtypeStruct((rows, width), jnp.bfloat16 if last else jnp.float32),
        compiler_params=pltpu.CompilerParams(vmem_limit_bytes=6 * 2**20),
        cost_estimate=pl.CostEstimate(flops=flops, bytes_accessed=2**10, transcendentals=0),
        name=name,
        **rest,
    )(*args)


def once_here(value, *others):
    anywhere = pl.BlockSpec(memory_space=pl.ANY)
    return pl.pallas_call(
        lambda *refs: None,
        in_specs=[anywhere] * (1 + len(others)),
        out_specs=anywhere,
        out_shape=jax.ShapeDtypeStruct(value.shape, value.dtype),
        input_output_aliases={0: 0},
        compiler_params=pltpu.CompilerParams(vmem_limit_bytes=2**20),
        cost_estimate=pl.CostEstimate(flops=0, bytes_accessed=0, transcendentals=0),
        name="once_here",
    )(value, *others)


def shards(queries, keys, values, doc_ids, out_weight):
    rows = keys.shape[0]
    shard = lax.axis_index("ctx")
    shard_count = lax.axis_size("ctx")
    places = lax.axis_size("head")
    other_core = [(i, i ^ 1) for i in range(shard_count)]

    def along_ctx(block, pairs):
        return lax.ppermute(block, "ctx", pairs)

    def along_head(block, step):
        return lax.ppermute(block, "head", [(i, (i + step) % places) for i in range(places)])

    own = jnp.concatenate([keys, values], 0)
    two_behind = along_ctx(own, [(i, i + 2) for i in range(shard_count - 2)])
    window = (REACH + 1) * rows
    padded = jnp.concatenate([jnp.full((REACH * rows,), -1, jnp.int32), doc_ids], 0)
    kdoc = lax.dynamic_slice_in_dim(padded, shard * rows, window, 0)
    kdoc = kdoc[None, :]

    splits = (0, 5)
    *state, qdoc, own_again = attend_own(queries, own, kdoc, splits)
    three_behind = along_ctx(own_again, [(i, i + 3) for i in range(1, shard_count - 3, 2)])
    beside = along_ctx(own_again, other_core)
    two_behind = once_here(two_behind, state[0])
    beside_two = along_ctx(two_behind, other_core)
    first_state = attend_two_behind(queries, two_behind, qdoc, kdoc, state[0:2])
    three_behind = once_here(three_behind, beside, beside_two, first_state[0])
    parts = (beside, two_behind, beside_two, three_behind)
    a, = attend_rest(queries, parts, qdoc, kdoc, first_state, splits[0], False)
    a_up = along_head(a, 1)
    a_down = along_head(a, -1)
    b, held = attend_rest(queries, parts, qdoc, kdoc, state[2:4], splits[1], True, out_weight)
    b_up = along_head(b, 1)
    b_down = along_head(b, -1)
    b_row = splits[1] * HEAD_SIZE
    up, down, across = places - 1, 1, places // 2
    total = project([a, b], [(0, 0), (0, b_row)], held, None, "project_own")
    a_up = once_here(a_up, total)
    a_far = along_head(a_up, 1)
    total = project([a_up, a_down], [(up, 0), (down, 0)], held, total, "project_a")
    b_down = once_here(b_down, b_up, total)
    b_far = along_head(b_down, -1)
    total = project([b_up, b_down], [(up, b_row), (down, b_row)], held, total, "project_b")
    total = project([b_far], [(across, b_row)], held, total, "project_b_far")
    return project([a_far], [(across, 0)], held, total, "project_a_far", last=True)


def solution(mesh):
    in_specs = (P("ctx", "head"), P("ctx", "head"), P("ctx", "head"), P(), P(None, "head"))
    out_specs = P("ctx", "head")
    return jax.shard_map(shards, mesh=mesh, in_specs=in_specs, out_specs=out_specs, check_vma=False)
```

```python
import functools
import math

import jax
import jax.numpy as jnp
from jax import lax
from jax.experimental import pallas as pl
from jax.experimental.pallas import tpu as pltpu
from jax.sharding import PartitionSpec as P

HEAD_SIZE = 128
REACH = 3
EXPONENT_SCALE = math.log2(math.e) * HEAD_SIZE ** (-0.5)
HIDDEN = -1e30
CONTRACT_LAST = (((1,), (1,)), ((), ()))
PLAIN = (((1,), (0,)), ((), ()))
VMEM = pl.BlockSpec(memory_space=pltpu.VMEM)
SMEM = pl.BlockSpec(memory_space=pltpu.SMEM)


def beside_ones(values):
    return jnp.concatenate([values, jnp.ones_like(values)], 1)


def wide(column, count):
    return column if count == 1 else jnp.concatenate([column] * count, 1)


def block_update(q, keys, values, bias, before, mixed):
    span = keys.shape[0]
    s = lax.dot_general(q, keys, CONTRACT_LAST, preferred_element_type=jnp.float32)
    if bias is not None:
        s = s + bias
    peak = jnp.broadcast_to(jnp.max(s, axis=1, keepdims=True), (q.shape[0], HEAD_SIZE))
    if before is not None:
        peak = jnp.maximum(before, peak)
    weights = jnp.exp2((s - wide(peak, span // HEAD_SIZE)) * EXPONENT_SCALE).astype(jnp.bfloat16)
    mix = lax.dot_general(weights, beside_ones(values), PLAIN, preferred_element_type=jnp.float32)
    if before is not None:
        mix = mix + mixed * wide(jnp.exp2((before - peak) * EXPONENT_SCALE), 2)
    return peak, mix


def own_kernel(splits, q_ref, own_ref, kdoc_ref, *refs):
    *states, qdoc_ref, again_ref, bias_ref = refs
    again_ref[...] = own_ref[...]
    rows = q_ref.shape[0]
    half = rows // 2
    heads = q_ref.shape[1] // HEAD_SIZE
    own_at = REACH * rows
    qdoc_ref[...] = jnp.broadcast_to(kdoc_ref[0:1, own_at:own_at + rows], (HEAD_SIZE, rows)).T
    for part in range(2):
        span = (part + 1) * half
        at = part * half
        row = at + lax.broadcasted_iota(jnp.int32, (half, span), 0)
        col = lax.broadcasted_iota(jnp.int32, (half, span), 1)
        doc = wide(qdoc_ref[at:at + half, :], span // HEAD_SIZE)
        seen = (doc == kdoc_ref[0:1, own_at:own_at + span]) & (col <= row)
        bias_ref[:, 0:span] = jnp.where(seen, 0.0, HIDDEN)
        for head in range(heads):
            q = q_ref[at:at + half, head * HEAD_SIZE:(head + 1) * HEAD_SIZE]
            peak, mix = block_update(q, own_ref[0:span, :], own_ref[rows:rows + span, :], bias_ref[:, 0:span], None, None)
            group = sum(head >= first for first in splits) - 1
            states[2 * group][head - splits[group], at:at + half, :] = peak
            states[2 * group + 1][head - splits[group], at:at + half, :] = mix


def update_seen(docs_ref, q_ref, qdoc_ref, kdoc_ref, bias_ref, blocks, states):
    rows = q_ref.shape[0]
    half = rows // 2

    own_at = REACH * rows

    def update(row_at, ref, shard, at, span, masked):
        here = pl.ds(row_at, half)
        keys = ref[pl.ds(at, span), :]
        values = ref[pl.ds(rows + at, span), :]
        if masked:
            doc = wide(qdoc_ref[here, :], span // HEAD_SIZE)
            window_at = pl.ds(pl.multiple_of(shard * rows + at, HEAD_SIZE), span)
            bias_ref[:, 0:span] = jnp.where(doc == kdoc_ref[0:1, window_at], 0.0, HIDDEN)
        for first_head, peak_ref, mix_ref in states:
            for head in range(peak_ref.shape[0]):
                column = (first_head + head) * HEAD_SIZE
                peak, mix = block_update(
                    q_ref[here, column:column + HEAD_SIZE], keys, values,
                    bias_ref[:, 0:span] if masked else None, peak_ref[head, here, :], mix_ref[head, here, :])
                peak_ref[head, here, :] = peak
                mix_ref[head, here, :] = mix

    @pl.loop(0, rows // half)
    def _(part):
        row_at = pl.multiple_of(part * half, half)
        first_doc = docs_ref[own_at + row_at]
        last_doc = docs_ref[own_at + row_at + half - 1]
        for ref, shard, span in blocks:
            @pl.loop(0, rows // span)
            def _(piece):
                at = pl.multiple_of(piece * span, span)
                lo, hi = docs_ref[shard * rows + at], docs_ref[shard * rows + at + span - 1]

                @pl.when((hi == first_doc) & (lo == last_doc))
                def _():
                    update(row_at, ref, shard, at, span, False)

                @pl.when((hi == first_doc) & (lo != last_doc))
                def _():
                    update(row_at, ref, shard, at, span, True)


def two_behind_kernel(docs_ref, q_ref, k2_ref, qdoc_ref, kdoc_ref, _, __, peak_ref, mix_ref, bias_ref):
    blocks = ((k2_ref, 1, q_ref.shape[0]),)
    update_seen(docs_ref, q_ref, qdoc_ref, kdoc_ref, bias_ref, blocks, ((0, peak_ref, mix_ref),))


def rest_kernel(first_head, heads, fetches, all_blocks, docs_ref, q_ref, beside_ref, k2_ref, beside_two_ref, three_ref,
                qdoc_ref, kdoc_ref, *refs):
    if fetches:
        weight_ref, _, _, peak_ref, mix_ref, out_ref, held_ref, bias_ref, k1_ref, k3_ref, fetched = refs
        fetch = pltpu.make_async_copy(weight_ref, held_ref, fetched)
        fetch.start()
    else:
        _, _, peak_ref, mix_ref, out_ref, bias_ref, k1_ref, k3_ref = refs
    rows = q_ref.shape[0]
    half = rows // 2
    second_core = lax.rem(lax.axis_index("ctx"), 2) == 1

    @pl.when(second_core)
    def _():
        k1_ref[...] = beside_ref[...]
        k3_ref[...] = beside_two_ref[...]

    @pl.when(jnp.logical_not(second_core))
    def _():
        k1_ref[...] = beside_two_ref[...]
        k3_ref[...] = three_ref[...]

    blocks = ((k1_ref, 2, rows), (k3_ref, 0, half))
    if all_blocks:
        blocks += ((k2_ref, 1, rows),)
    update_seen(docs_ref, q_ref, qdoc_ref, kdoc_ref, bias_ref, blocks, ((first_head, peak_ref, mix_ref),))
    for head in range(heads):
        mix = mix_ref[head, :, 0:HEAD_SIZE] / mix_ref[head, :, HEAD_SIZE:]
        out_ref[:, head * HEAD_SIZE:(head + 1) * HEAD_SIZE] = mix.astype(jnp.bfloat16)
    if fetches:
        fetch.wait()


def state_shapes(heads, rows):
    return [
        jax.ShapeDtypeStruct((heads, rows, HEAD_SIZE), jnp.float32),
        jax.ShapeDtypeStruct((heads, rows, 2 * HEAD_SIZE), jnp.float32),
    ]


ATTEND_COST = pl.CostEstimate(flops=2**32, bytes_accessed=2**20, transcendentals=2**20)


def attend_own(queries, own, kdoc, splits):
    rows, width = queries.shape
    ends = splits[1:] + (width // HEAD_SIZE,)
    return pl.pallas_call(
        functools.partial(own_kernel, splits),
        in_specs=[VMEM] * 3,
        out_specs=[VMEM] * (2 * len(splits) + 2),
        scratch_shapes=[pltpu.VMEM((rows // 2, rows), jnp.float32)],
        out_shape=[shape for first, end in zip(splits, ends) for shape in state_shapes(end - first, rows)]
        + [jax.ShapeDtypeStruct((rows, HEAD_SIZE), jnp.int32), jax.ShapeDtypeStruct(own.shape, own.dtype)],
        compiler_params=pltpu.CompilerParams(vmem_limit_bytes=8 * 2**20),
        cost_estimate=ATTEND_COST,
        name="attend_own",
    )(queries, own, kdoc)


def attend_two_behind(queries, block, qdoc, kdoc, state):
    rows = queries.shape[0]
    return pl.pallas_call(
        two_behind_kernel,
        in_specs=[SMEM] + [VMEM] * 6,
        out_specs=[VMEM] * 2,
        scratch_shapes=[pltpu.VMEM((rows // 2, rows), jnp.float32)],
        out_shape=state_shapes(state[0].shape[0], rows),
        input_output_aliases={5: 0, 6: 1},
        compiler_params=pltpu.CompilerParams(vmem_limit_bytes=8 * 2**20),
        cost_estimate=ATTEND_COST,
        name="attend_two_behind",
    )(kdoc.reshape(-1), queries, block, qdoc, kdoc, *state)


def attend_rest(queries, parts, qdoc, kdoc, state, first_head, all_blocks, weight=None):
    rows = queries.shape[0]
    heads = state[0].shape[0]
    fetches = weight is not None
    attended = jax.ShapeDtypeStruct((rows, heads * HEAD_SIZE), jnp.bfloat16)
    return pl.pallas_call(
        functools.partial(rest_kernel, first_head, heads, fetches, all_blocks),
        in_specs=[SMEM] + [VMEM] * 7 + [pl.BlockSpec(memory_space=pl.ANY)] * fetches + [VMEM] * 2,
        out_specs=[VMEM] * (3 + fetches),
        scratch_shapes=[
            pltpu.VMEM((rows // 2, rows), jnp.float32),
            pltpu.VMEM(parts[0].shape, jnp.bfloat16),
            pltpu.VMEM(parts[0].shape, jnp.bfloat16),
        ] + [pltpu.SemaphoreType.DMA] * fetches,
        out_shape=state_shapes(heads, rows) + [attended]
        + ([jax.ShapeDtypeStruct(weight.shape, weight.dtype)] if fetches else []),
        input_output_aliases={8 + fetches: 0, 9 + fetches: 1},
        compiler_params=pltpu.CompilerParams(vmem_limit_bytes=(24 if fetches else 8) * 2**20),
        cost_estimate=ATTEND_COST,
        name=f"attend_rest_{first_head}",
    )(kdoc.reshape(-1), queries, *parts, qdoc, kdoc, *[weight] * fetches, *state)[2:]


def project_kernel(count, carried, columns, starts, *refs):
    weight_ref, out_ref = refs[count], refs[-1]
    places = lax.axis_size("head")
    share = weight_ref.shape[0] // places
    tiled = out_ref.shape[1] < weight_ref.shape[1]
    for step in [pl.program_id(0)] if tiled else range(weight_ref.shape[1] // columns):
        here = pl.ds(pl.multiple_of(step * columns, columns), columns)
        total = refs[count + 1][:, here] if carried else None
        for i in range(count):
            hops, first_row = starts[i]
            place = lax.rem(lax.axis_index("head") + hops, places)
            rows = pl.ds(pl.multiple_of(place * share + first_row, HEAD_SIZE), refs[i].shape[1])
            term = lax.dot_general(refs[i][...], weight_ref[rows, here], PLAIN, preferred_element_type=jnp.float32)
            total = term if total is None else total + term
        out_ref[:, slice(None) if tiled else here] = total.astype(out_ref.dtype)


def project(pieces, starts, weight, total, name, last=False, columns=512, flops=2**20):
    rows, width = pieces[0].shape[0], weight.shape[1]
    carried = total is not None
    args = [*pieces, weight] + [total] * carried
    if last:
        rest = dict(grid=(width // columns,), out_specs=pl.BlockSpec((rows, columns), lambda n: (0, n)))
    else:
        rest = dict(out_specs=VMEM, input_output_aliases={len(args) - 1: 0} if carried else {})
    return pl.pallas_call(
        functools.partial(project_kernel, len(pieces), carried, columns, starts),
        in_specs=[VMEM] * len(args),
        out_shape=jax.ShapeDtypeStruct((rows, width), jnp.bfloat16 if last else jnp.float32),
        compiler_params=pltpu.CompilerParams(vmem_limit_bytes=6 * 2**20),
        cost_estimate=pl.CostEstimate(flops=flops, bytes_accessed=2**10, transcendentals=0),
        name=name,
        **rest,
    )(*args)


def once_here(value, *others):
    anywhere = pl.BlockSpec(memory_space=pl.ANY)
    return pl.pallas_call(
        lambda *refs: None,
        in_specs=[anywhere] * (1 + len(others)),
        out_specs=anywhere,
        out_shape=jax.ShapeDtypeStruct(value.shape, value.dtype),
        input_output_aliases={0: 0},
        compiler_params=pltpu.CompilerParams(vmem_limit_bytes=2**20),
        cost_estimate=pl.CostEstimate(flops=0, bytes_accessed=0, transcendentals=0),
        name="once_here",
    )(value, *others)


def shards(queries, keys, values, doc_ids, out_weight):
    rows = keys.shape[0]
    shard = lax.axis_index("ctx")
    shard_count = lax.axis_size("ctx")
    places = lax.axis_size("head")
    other_core = [(i, i ^ 1) for i in range(shard_count)]

    def along_ctx(block, pairs):
        return lax.ppermute(block, "ctx", pairs)

    def along_head(block, step):
        return lax.ppermute(block, "head", [(i, (i + step) % places) for i in range(places)])

    own = jnp.concatenate([keys, values], 0)
    two_behind = along_ctx(own, [(i, i + 2) for i in range(shard_count - 2)])
    window = (REACH + 1) * rows
    padded = jnp.concatenate([jnp.full((REACH * rows,), -1, jnp.int32), doc_ids], 0)
    kdoc = lax.dynamic_slice_in_dim(padded, shard * rows, window, 0)
    kdoc = kdoc[None, :]

    splits = (0, 5)
    *state, qdoc, own_again = attend_own(queries, own, kdoc, splits)
    three_behind = along_ctx(own_again, [(i, i + 3) for i in range(1, shard_count - 3, 2)])
    beside = along_ctx(own_again, other_core)
    two_behind = once_here(two_behind, state[0])
    beside_two = along_ctx(two_behind, other_core)
    first_state = attend_two_behind(queries, two_behind, qdoc, kdoc, state[0:2])
    three_behind = once_here(three_behind, beside, beside_two, first_state[0])
    parts = (beside, two_behind, beside_two, three_behind)
    a, = attend_rest(queries, parts, qdoc, kdoc, first_state, splits[0], False)
    a_up = along_head(a, 1)
    a_down = along_head(a, -1)
    b, held = attend_rest(queries, parts, qdoc, kdoc, state[2:4], splits[1], True, out_weight)
    b_up = along_head(b, 1)
    b_down = along_head(b, -1)
    b_row = splits[1] * HEAD_SIZE
    up, down, across = places - 1, 1, places // 2
    total = project([a, b], [(0, 0), (0, b_row)], held, None, "project_own")
    a_up = once_here(a_up, total)
    a_far = along_head(a_up, 1)
    total = project([a_up, a_down], [(up, 0), (down, 0)], held, total, "project_a")
    b_down = once_here(b_down, b_up, total)
    b_far = along_head(b_down, -1)
    total = project([b_up, b_down], [(up, b_row), (down, b_row)], held, total, "project_b")
    total = project([b_far], [(across, b_row)], held, total, "project_b_far")
    return project([a_far], [(across, 0)], held, total, "project_a_far", last=True, columns=1024)


def solution(mesh):
    in_specs = (P("ctx", "head"), P("ctx", "head"), P("ctx", "head"), P(), P(None, "head"))
    out_specs = P("ctx", "head")
    return jax.shard_map(shards, mesh=mesh, in_specs=in_specs, out_specs=out_specs, check_vma=False)
```

```python
import functools
import math

import jax
import jax.numpy as jnp
from jax import lax
from jax.experimental import pallas as pl
from jax.experimental.pallas import tpu as pltpu
from jax.sharding import PartitionSpec as P

HEAD_SIZE = 128
REACH = 3
EXPONENT_SCALE = math.log2(math.e) * HEAD_SIZE ** (-0.5)
HIDDEN = -1e30
CONTRACT_LAST = (((1,), (1,)), ((), ()))
PLAIN = (((1,), (0,)), ((), ()))
VMEM = pl.BlockSpec(memory_space=pltpu.VMEM)
SMEM = pl.BlockSpec(memory_space=pltpu.SMEM)


def beside_ones(values):
    return jnp.concatenate([values, jnp.ones_like(values)], 1)


def wide(column, count):
    return column if count == 1 else jnp.concatenate([column] * count, 1)


def block_update(q, keys, values, bias, before, mixed):
    span = keys.shape[0]
    s = lax.dot_general(q, keys, CONTRACT_LAST, preferred_element_type=jnp.float32)
    if bias is not None:
        s = s + bias
    peak = jnp.broadcast_to(jnp.max(s, axis=1, keepdims=True), (q.shape[0], HEAD_SIZE))
    if before is not None:
        peak = jnp.maximum(before, peak)
    weights = jnp.exp2((s - wide(peak, span // HEAD_SIZE)) * EXPONENT_SCALE).astype(jnp.bfloat16)
    mix = lax.dot_general(weights, beside_ones(values), PLAIN, preferred_element_type=jnp.float32)
    if before is not None:
        mix = mix + mixed * wide(jnp.exp2((before - peak) * EXPONENT_SCALE), 2)
    return peak, mix


def own_kernel(splits, q_ref, own_ref, kdoc_ref, *refs):
    *states, qdoc_ref, again_ref, bias_ref = refs
    again_ref[...] = own_ref[...]
    rows = q_ref.shape[0]
    half = rows // 2
    heads = q_ref.shape[1] // HEAD_SIZE
    own_at = REACH * rows
    qdoc_ref[...] = jnp.broadcast_to(kdoc_ref[0:1, own_at:own_at + rows], (HEAD_SIZE, rows)).T
    for part in range(2):
        span = (part + 1) * half
        at = part * half
        row = at + lax.broadcasted_iota(jnp.int32, (half, span), 0)
        col = lax.broadcasted_iota(jnp.int32, (half, span), 1)
        doc = wide(qdoc_ref[at:at + half, :], span // HEAD_SIZE)
        seen = (doc == kdoc_ref[0:1, own_at:own_at + span]) & (col <= row)
        bias_ref[:, 0:span] = jnp.where(seen, 0.0, HIDDEN)
        for head in range(heads):
            q = q_ref[at:at + half, head * HEAD_SIZE:(head + 1) * HEAD_SIZE]
            peak, mix = block_update(q, own_ref[0:span, :], own_ref[rows:rows + span, :], bias_ref[:, 0:span], None, None)
            group = sum(head >= first for first in splits) - 1
            states[2 * group][head - splits[group], at:at + half, :] = peak
            states[2 * group + 1][head - splits[group], at:at + half, :] = mix


def update_seen(docs_ref, q_ref, qdoc_ref, kdoc_ref, bias_ref, blocks, states):
    rows = q_ref.shape[0]
    half = rows // 2

    own_at = REACH * rows

    def update(row_at, ref, shard, at, span, masked):
        here = pl.ds(row_at, half)
        keys = ref[pl.ds(at, span), :]
        values = ref[pl.ds(rows + at, span), :]
        if masked:
            doc = wide(qdoc_ref[here, :], span // HEAD_SIZE)
            window_at = pl.ds(pl.multiple_of(shard * rows + at, HEAD_SIZE), span)
            bias_ref[:, 0:span] = jnp.where(doc == kdoc_ref[0:1, window_at], 0.0, HIDDEN)
        for first_head, peak_ref, mix_ref in states:
            for head in range(peak_ref.shape[0]):
                column = (first_head + head) * HEAD_SIZE
                peak, mix = block_update(
                    q_ref[here, column:column + HEAD_SIZE], keys, values,
                    bias_ref[:, 0:span] if masked else None, peak_ref[head, here, :], mix_ref[head, here, :])
                peak_ref[head, here, :] = peak
                mix_ref[head, here, :] = mix

    @pl.loop(0, rows // half)
    def _(part):
        row_at = pl.multiple_of(part * half, half)
        first_doc = docs_ref[own_at + row_at]
        last_doc = docs_ref[own_at + row_at + half - 1]
        for ref, shard, span in blocks:
            @pl.loop(0, rows // span)
            def _(piece):
                at = pl.multiple_of(piece * span, span)
                lo, hi = docs_ref[shard * rows + at], docs_ref[shard * rows + at + span - 1]

                @pl.when((hi == first_doc) & (lo == last_doc))
                def _():
                    update(row_at, ref, shard, at, span, False)

                @pl.when((hi == first_doc) & (lo != last_doc))
                def _():
                    update(row_at, ref, shard, at, span, True)


def two_behind_kernel(docs_ref, q_ref, k2_ref, qdoc_ref, kdoc_ref, _, __, peak_ref, mix_ref, bias_ref):
    blocks = ((k2_ref, 1, q_ref.shape[0]),)
    update_seen(docs_ref, q_ref, qdoc_ref, kdoc_ref, bias_ref, blocks, ((0, peak_ref, mix_ref),))


def rest_kernel(first_head, heads, fetches, all_blocks, docs_ref, q_ref, beside_ref, k2_ref, beside_two_ref, three_ref,
                qdoc_ref, kdoc_ref, *refs):
    if fetches:
        weight_ref, _, _, peak_ref, mix_ref, out_ref, held_ref, bias_ref, k1_ref, k3_ref, fetched = refs
        fetch = pltpu.make_async_copy(weight_ref, held_ref, fetched)
        fetch.start()
    else:
        _, _, peak_ref, mix_ref, out_ref, bias_ref, k1_ref, k3_ref = refs
    rows = q_ref.shape[0]
    half = rows // 2
    second_core = lax.rem(lax.axis_index("ctx"), 2) == 1

    @pl.when(second_core)
    def _():
        k1_ref[...] = beside_ref[...]
        k3_ref[...] = beside_two_ref[...]

    @pl.when(jnp.logical_not(second_core))
    def _():
        k1_ref[...] = beside_two_ref[...]
        k3_ref[...] = three_ref[...]

    blocks = ((k1_ref, 2, rows), (k3_ref, 0, half))
    if all_blocks:
        blocks += ((k2_ref, 1, rows),)
    update_seen(docs_ref, q_ref, qdoc_ref, kdoc_ref, bias_ref, blocks, ((first_head, peak_ref, mix_ref),))
    for head in range(heads):
        mix = mix_ref[head, :, 0:HEAD_SIZE] / mix_ref[head, :, HEAD_SIZE:]
        out_ref[:, head * HEAD_SIZE:(head + 1) * HEAD_SIZE] = mix.astype(jnp.bfloat16)
    if fetches:
        fetch.wait()


def state_shapes(heads, rows):
    return [
        jax.ShapeDtypeStruct((heads, rows, HEAD_SIZE), jnp.float32),
        jax.ShapeDtypeStruct((heads, rows, 2 * HEAD_SIZE), jnp.float32),
    ]


ATTEND_COST = pl.CostEstimate(flops=2**32, bytes_accessed=2**20, transcendentals=2**20)


def attend_own(queries, own, kdoc, splits):
    rows, width = queries.shape
    ends = splits[1:] + (width // HEAD_SIZE,)
    return pl.pallas_call(
        functools.partial(own_kernel, splits),
        in_specs=[VMEM] * 3,
        out_specs=[VMEM] * (2 * len(splits) + 2),
        scratch_shapes=[pltpu.VMEM((rows // 2, rows), jnp.float32)],
        out_shape=[shape for first, end in zip(splits, ends) for shape in state_shapes(end - first, rows)]
        + [jax.ShapeDtypeStruct((rows, HEAD_SIZE), jnp.int32), jax.ShapeDtypeStruct(own.shape, own.dtype)],
        compiler_params=pltpu.CompilerParams(vmem_limit_bytes=8 * 2**20),
        cost_estimate=ATTEND_COST,
        name="attend_own",
    )(queries, own, kdoc)


def attend_two_behind(queries, block, qdoc, kdoc, state):
    rows = queries.shape[0]
    return pl.pallas_call(
        two_behind_kernel,
        in_specs=[SMEM] + [VMEM] * 6,
        out_specs=[VMEM] * 2,
        scratch_shapes=[pltpu.VMEM((rows // 2, rows), jnp.float32)],
        out_shape=state_shapes(state[0].shape[0], rows),
        input_output_aliases={5: 0, 6: 1},
        compiler_params=pltpu.CompilerParams(vmem_limit_bytes=8 * 2**20),
        cost_estimate=ATTEND_COST,
        name="attend_two_behind",
    )(kdoc.reshape(-1), queries, block, qdoc, kdoc, *state)


def attend_rest(queries, parts, qdoc, kdoc, state, first_head, all_blocks, weight=None):
    rows = queries.shape[0]
    heads = state[0].shape[0]
    fetches = weight is not None
    attended = jax.ShapeDtypeStruct((rows, heads * HEAD_SIZE), jnp.bfloat16)
    return pl.pallas_call(
        functools.partial(rest_kernel, first_head, heads, fetches, all_blocks),
        in_specs=[SMEM] + [VMEM] * 7 + [pl.BlockSpec(memory_space=pl.ANY)] * fetches + [VMEM] * 2,
        out_specs=[VMEM] * (3 + fetches),
        scratch_shapes=[
            pltpu.VMEM((rows // 2, rows), jnp.float32),
            pltpu.VMEM(parts[0].shape, jnp.bfloat16),
            pltpu.VMEM(parts[0].shape, jnp.bfloat16),
        ] + [pltpu.SemaphoreType.DMA] * fetches,
        out_shape=state_shapes(heads, rows) + [attended]
        + ([jax.ShapeDtypeStruct(weight.shape, weight.dtype)] if fetches else []),
        input_output_aliases={8 + fetches: 0, 9 + fetches: 1},
        compiler_params=pltpu.CompilerParams(vmem_limit_bytes=(24 if fetches else 8) * 2**20),
        cost_estimate=ATTEND_COST,
        name=f"attend_rest_{first_head}",
    )(kdoc.reshape(-1), queries, *parts, qdoc, kdoc, *[weight] * fetches, *state)[2:]


def project_kernel(count, carried, last, columns, starts, *refs):
    weight_ref, out_ref = refs[count], refs[count + 1 + carried]
    places = lax.axis_size("head")
    share = weight_ref.shape[0] // places
    copies = []
    for step in range(weight_ref.shape[1] // columns):
        here = slice(step * columns, (step + 1) * columns)
        total = refs[count + 1][:, here] if carried else None
        for i in range(count):
            hops, first_row = starts[i]
            place = lax.rem(lax.axis_index("head") + hops, places)
            rows = pl.ds(pl.multiple_of(place * share + first_row, HEAD_SIZE), refs[i].shape[1])
            term = lax.dot_general(refs[i][...], weight_ref[rows, here], PLAIN, preferred_element_type=jnp.float32)
            total = term if total is None else total + term
        if last:
            tile_ref, sems = refs[-2], refs[-1]
            tile_ref[step] = total.astype(out_ref.dtype)
            copies.append(pltpu.make_async_copy(tile_ref.at[step], out_ref.at[:, here], sems.at[step]))
            copies[-1].start()
        else:
            out_ref[:, here] = total
    for copy in copies:
        copy.wait()


def project(pieces, starts, weight, total, name, last=False, columns=512, flops=2**20):
    rows, width = pieces[0].shape[0], weight.shape[1]
    carried = total is not None
    args = [*pieces, weight] + [total] * carried
    tiles = width // columns
    if last:
        rest = dict(
            out_specs=pl.BlockSpec(memory_space=pl.ANY),
            scratch_shapes=[pltpu.VMEM((tiles, rows, columns), jnp.bfloat16), pltpu.SemaphoreType.DMA((tiles,))],
        )
    else:
        rest = dict(out_specs=VMEM, input_output_aliases={len(args) - 1: 0} if carried else {})
    return pl.pallas_call(
        functools.partial(project_kernel, len(pieces), carried, last, columns, starts),
        in_specs=[VMEM] * len(args),
        out_shape=jax.ShapeDtypeStruct((rows, width), jnp.bfloat16 if last else jnp.float32),
        compiler_params=pltpu.CompilerParams(vmem_limit_bytes=6 * 2**20),
        cost_estimate=pl.CostEstimate(flops=flops, bytes_accessed=2**10, transcendentals=0),
        name=name,
        **rest,
    )(*args)


def once_here(value, *others):
    anywhere = pl.BlockSpec(memory_space=pl.ANY)
    return pl.pallas_call(
        lambda *refs: None,
        in_specs=[anywhere] * (1 + len(others)),
        out_specs=anywhere,
        out_shape=jax.ShapeDtypeStruct(value.shape, value.dtype),
        input_output_aliases={0: 0},
        compiler_params=pltpu.CompilerParams(vmem_limit_bytes=2**20),
        cost_estimate=pl.CostEstimate(flops=0, bytes_accessed=0, transcendentals=0),
        name="once_here",
    )(value, *others)


def shards(queries, keys, values, doc_ids, out_weight):
    rows = keys.shape[0]
    shard = lax.axis_index("ctx")
    shard_count = lax.axis_size("ctx")
    places = lax.axis_size("head")
    other_core = [(i, i ^ 1) for i in range(shard_count)]

    def along_ctx(block, pairs):
        return lax.ppermute(block, "ctx", pairs)

    def along_head(block, step):
        return lax.ppermute(block, "head", [(i, (i + step) % places) for i in range(places)])

    own = jnp.concatenate([keys, values], 0)
    two_behind = along_ctx(own, [(i, i + 2) for i in range(shard_count - 2)])
    three_behind = along_ctx(own, [(i, i + 3) for i in range(1, shard_count - 3, 2)])
    window = (REACH + 1) * rows
    padded = jnp.concatenate([jnp.full((REACH * rows,), -1, jnp.int32), doc_ids], 0)
    kdoc = lax.dynamic_slice_in_dim(padded, shard * rows, window, 0)
    kdoc = kdoc[None, :]

    splits = (0, 5)
    *state, qdoc, own_again = attend_own(queries, own, kdoc, splits)
    beside = along_ctx(own_again, other_core)
    two_behind = once_here(two_behind, state[0])
    beside_two = along_ctx(two_behind, other_core)
    first_state = attend_two_behind(queries, two_behind, qdoc, kdoc, state[0:2])
    three_behind = once_here(three_behind, beside, beside_two, first_state[0])
    parts = (beside, two_behind, beside_two, three_behind)
    a, = attend_rest(queries, parts, qdoc, kdoc, first_state, splits[0], False)
    a_up = along_head(a, 1)
    a_down = along_head(a, -1)
    b, held = attend_rest(queries, parts, qdoc, kdoc, state[2:4], splits[1], True, out_weight)
    b_up = along_head(b, 1)
    b_down = along_head(b, -1)
    b_row = splits[1] * HEAD_SIZE
    up, down, across = places - 1, 1, places // 2
    total = project([a, b], [(0, 0), (0, b_row)], held, None, "project_own")
    a_up = once_here(a_up, total)
    a_far = along_head(a_up, 1)
    total = project([a_up, a_down], [(up, 0), (down, 0)], held, total, "project_a")
    b_down = once_here(b_down, b_up, total)
    b_far = along_head(b_down, -1)
    total = project([b_up, b_down], [(up, b_row), (down, b_row)], held, total, "project_b")
    total = project([b_far], [(across, b_row)], held, total, "project_b_far")
    return project([a_far], [(across, 0)], held, total, "project_a_far", last=True)


def solution(mesh):
    in_specs = (P("ctx", "head"), P("ctx", "head"), P("ctx", "head"), P(), P(None, "head"))
    out_specs = P("ctx", "head")
    return jax.shard_map(shards, mesh=mesh, in_specs=in_specs, out_specs=out_specs, check_vma=False)
```

```python
import functools
import math

import jax
import jax.numpy as jnp
from jax import lax
from jax.experimental import pallas as pl
from jax.experimental.pallas import tpu as pltpu
from jax.sharding import PartitionSpec as P

HEAD_SIZE = 128
REACH = 3
EXPONENT_SCALE = math.log2(math.e) * HEAD_SIZE ** (-0.5)
HIDDEN = -1e30
CONTRACT_LAST = (((1,), (1,)), ((), ()))
PLAIN = (((1,), (0,)), ((), ()))
VMEM = pl.BlockSpec(memory_space=pltpu.VMEM)
SMEM = pl.BlockSpec(memory_space=pltpu.SMEM)


def beside_ones(values):
    return jnp.concatenate([values, jnp.ones_like(values)], 1)


def wide(column, count):
    return column if count == 1 else jnp.concatenate([column] * count, 1)


def block_update(q, keys, values, bias, before, mixed):
    span = keys.shape[0]
    s = lax.dot_general(q, keys, CONTRACT_LAST, preferred_element_type=jnp.float32)
    if bias is not None:
        s = s + bias
    peak = jnp.broadcast_to(jnp.max(s, axis=1, keepdims=True), (q.shape[0], HEAD_SIZE))
    if before is not None:
        peak = jnp.maximum(before, peak)
    weights = jnp.exp2((s - wide(peak, span // HEAD_SIZE)) * EXPONENT_SCALE).astype(jnp.bfloat16)
    mix = lax.dot_general(weights, beside_ones(values), PLAIN, preferred_element_type=jnp.float32)
    if before is not None:
        mix = mix + mixed * wide(jnp.exp2((before - peak) * EXPONENT_SCALE), 2)
    return peak, mix


def begin_states(q_ref, own_ref, qdoc_ref, kdoc_ref, bias_ref, first_head, peak_ref, mix_ref):
    rows = q_ref.shape[0]
    half = rows // 2
    own_at = REACH * rows
    for part in range(2):
        span = (part + 1) * half
        at = part * half
        row = at + lax.broadcasted_iota(jnp.int32, (half, span), 0)
        col = lax.broadcasted_iota(jnp.int32, (half, span), 1)
        doc = wide(qdoc_ref[at:at + half, :], span // HEAD_SIZE)
        seen = (doc == kdoc_ref[0:1, own_at:own_at + span]) & (col <= row)
        bias_ref[:, 0:span] = jnp.where(seen, 0.0, HIDDEN)
        for head in range(peak_ref.shape[0]):
            column = (first_head + head) * HEAD_SIZE
            q = q_ref[at:at + half, column:column + HEAD_SIZE]
            peak, mix = block_update(q, own_ref[0:span, :], own_ref[rows:rows + span, :], bias_ref[:, 0:span], None, None)
            peak_ref[head, at:at + half, :] = peak
            mix_ref[head, at:at + half, :] = mix


def own_kernel(q_ref, own_ref, kdoc_ref, peak_ref, mix_ref, qdoc_ref, again_ref, bias_ref):
    rows = q_ref.shape[0]
    own_at = REACH * rows
    again_ref[...] = own_ref[...]
    qdoc_ref[...] = jnp.broadcast_to(kdoc_ref[0:1, own_at:own_at + rows], (HEAD_SIZE, rows)).T
    begin_states(q_ref, own_ref, qdoc_ref, kdoc_ref, bias_ref, 0, peak_ref, mix_ref)


def update_seen(docs_ref, q_ref, qdoc_ref, kdoc_ref, bias_ref, blocks, states):
    rows = q_ref.shape[0]
    half = rows // 2

    own_at = REACH * rows

    def update(row_at, ref, shard, at, span, masked):
        here = pl.ds(row_at, half)
        keys = ref[pl.ds(at, span), :]
        values = ref[pl.ds(rows + at, span), :]
        if masked:
            doc = wide(qdoc_ref[here, :], span // HEAD_SIZE)
            window_at = pl.ds(pl.multiple_of(shard * rows + at, HEAD_SIZE), span)
            bias_ref[:, 0:span] = jnp.where(doc == kdoc_ref[0:1, window_at], 0.0, HIDDEN)
        for first_head, peak_ref, mix_ref in states:
            for head in range(peak_ref.shape[0]):
                column = (first_head + head) * HEAD_SIZE
                peak, mix = block_update(
                    q_ref[here, column:column + HEAD_SIZE], keys, values,
                    bias_ref[:, 0:span] if masked else None, peak_ref[head, here, :], mix_ref[head, here, :])
                peak_ref[head, here, :] = peak
                mix_ref[head, here, :] = mix

    @pl.loop(0, rows // half)
    def _(part):
        row_at = pl.multiple_of(part * half, half)
        first_doc = docs_ref[own_at + row_at]
        last_doc = docs_ref[own_at + row_at + half - 1]
        for ref, shard, span in blocks:
            @pl.loop(0, rows // span)
            def _(piece):
                at = pl.multiple_of(piece * span, span)
                lo, hi = docs_ref[shard * rows + at], docs_ref[shard * rows + at + span - 1]

                @pl.when((hi == first_doc) & (lo == last_doc))
                def _():
                    update(row_at, ref, shard, at, span, False)

                @pl.when((hi == first_doc) & (lo != last_doc))
                def _():
                    update(row_at, ref, shard, at, span, True)


def two_behind_kernel(docs_ref, q_ref, k2_ref, qdoc_ref, kdoc_ref, _, __, peak_ref, mix_ref, bias_ref):
    blocks = ((k2_ref, 1, q_ref.shape[0]),)
    update_seen(docs_ref, q_ref, qdoc_ref, kdoc_ref, bias_ref, blocks, ((0, peak_ref, mix_ref),))


def rest_kernel(first_head, heads, begun, docs_ref, q_ref, beside_ref, k2_ref, beside_two_ref, three_ref,
                qdoc_ref, kdoc_ref, *refs):
    if begun:
        _, _, peak_ref, mix_ref, out_ref, bias_ref, k1_ref, k3_ref = refs
    else:
        own_ref, weight_ref, out_ref, held_ref, peak_ref, mix_ref, bias_ref, k1_ref, k3_ref, fetched = refs
        fetch = pltpu.make_async_copy(weight_ref, held_ref, fetched)
        fetch.start()
        begin_states(q_ref, own_ref, qdoc_ref, kdoc_ref, bias_ref, first_head, peak_ref, mix_ref)
    rows = q_ref.shape[0]
    half = rows // 2
    second_core = lax.rem(lax.axis_index("ctx"), 2) == 1

    @pl.when(second_core)
    def _():
        k1_ref[...] = beside_ref[...]
        k3_ref[...] = beside_two_ref[...]

    @pl.when(jnp.logical_not(second_core))
    def _():
        k1_ref[...] = beside_two_ref[...]
        k3_ref[...] = three_ref[...]

    blocks = ((k1_ref, 2, rows), (k3_ref, 0, half))
    if not begun:
        blocks += ((k2_ref, 1, rows),)
    update_seen(docs_ref, q_ref, qdoc_ref, kdoc_ref, bias_ref, blocks, ((first_head, peak_ref, mix_ref),))
    for head in range(heads):
        mix = mix_ref[head, :, 0:HEAD_SIZE] / mix_ref[head, :, HEAD_SIZE:]
        out_ref[:, head * HEAD_SIZE:(head + 1) * HEAD_SIZE] = mix.astype(jnp.bfloat16)
    if not begun:
        fetch.wait()


def state_shapes(heads, rows):
    return [
        jax.ShapeDtypeStruct((heads, rows, HEAD_SIZE), jnp.float32),
        jax.ShapeDtypeStruct((heads, rows, 2 * HEAD_SIZE), jnp.float32),
    ]


ATTEND_COST = pl.CostEstimate(flops=2**32, bytes_accessed=2**20, transcendentals=2**20)


def attend_own(queries, own, kdoc, heads):
    rows = queries.shape[0]
    return pl.pallas_call(
        own_kernel,
        in_specs=[VMEM] * 3,
        out_specs=[VMEM] * 4,
        scratch_shapes=[pltpu.VMEM((rows // 2, rows), jnp.float32)],
        out_shape=state_shapes(heads, rows)
        + [jax.ShapeDtypeStruct((rows, HEAD_SIZE), jnp.int32), jax.ShapeDtypeStruct(own.shape, own.dtype)],
        compiler_params=pltpu.CompilerParams(vmem_limit_bytes=8 * 2**20),
        cost_estimate=ATTEND_COST,
        name="attend_own",
    )(queries, own, kdoc)


def attend_two_behind(queries, block, qdoc, kdoc, state):
    rows = queries.shape[0]
    return pl.pallas_call(
        two_behind_kernel,
        in_specs=[SMEM] + [VMEM] * 6,
        out_specs=[VMEM] * 2,
        scratch_shapes=[pltpu.VMEM((rows // 2, rows), jnp.float32)],
        out_shape=state_shapes(state[0].shape[0], rows),
        input_output_aliases={5: 0, 6: 1},
        compiler_params=pltpu.CompilerParams(vmem_limit_bytes=8 * 2**20),
        cost_estimate=ATTEND_COST,
        name="attend_two_behind",
    )(kdoc.reshape(-1), queries, block, qdoc, kdoc, *state)


def attend_rest(queries, parts, qdoc, kdoc, state):
    rows = queries.shape[0]
    heads = state[0].shape[0]
    return pl.pallas_call(
        functools.partial(rest_kernel, 0, heads, True),
        in_specs=[SMEM] + [VMEM] * 9,
        out_specs=[VMEM] * 3,
        scratch_shapes=[
            pltpu.VMEM((rows // 2, rows), jnp.float32),
            pltpu.VMEM(parts[0].shape, jnp.bfloat16),
            pltpu.VMEM(parts[0].shape, jnp.bfloat16),
        ],
        out_shape=state_shapes(heads, rows) + [jax.ShapeDtypeStruct((rows, heads * HEAD_SIZE), jnp.bfloat16)],
        input_output_aliases={8: 0, 9: 1},
        compiler_params=pltpu.CompilerParams(vmem_limit_bytes=8 * 2**20),
        cost_estimate=ATTEND_COST,
        name="attend_rest",
    )(kdoc.reshape(-1), queries, *parts, qdoc, kdoc, *state)[2]


def attend_whole(queries, parts, qdoc, kdoc, own, first_head, weight):
    rows, width = queries.shape
    heads = width // HEAD_SIZE - first_head
    return pl.pallas_call(
        functools.partial(rest_kernel, first_head, heads, False),
        in_specs=[SMEM] + [VMEM] * 8 + [pl.BlockSpec(memory_space=pl.ANY)],
        out_specs=[VMEM] * 2,
        scratch_shapes=[pltpu.VMEM(shape.shape, shape.dtype) for shape in state_shapes(heads, rows)] + [
            pltpu.VMEM((rows // 2, rows), jnp.float32),
            pltpu.VMEM(parts[0].shape, jnp.bfloat16),
            pltpu.VMEM(parts[0].shape, jnp.bfloat16),
            pltpu.SemaphoreType.DMA,
        ],
        out_shape=[
            jax.ShapeDtypeStruct((rows, heads * HEAD_SIZE), jnp.bfloat16),
            jax.ShapeDtypeStruct(weight.shape, weight.dtype),
        ],
        compiler_params=pltpu.CompilerParams(vmem_limit_bytes=26 * 2**20),
        cost_estimate=ATTEND_COST,
        name="attend_whole",
    )(kdoc.reshape(-1), queries, *parts, qdoc, kdoc, own, weight)


def project_kernel(count, carried, last, columns, starts, *refs):
    weight_ref, out_ref = refs[count], refs[count + 1 + carried]
    places = lax.axis_size("head")
    share = weight_ref.shape[0] // places
    copies = []
    for step in range(weight_ref.shape[1] // columns):
        here = slice(step * columns, (step + 1) * columns)
        total = refs[count + 1][:, here] if carried else None
        for i in range(count):
            hops, first_row = starts[i]
            place = lax.rem(lax.axis_index("head") + hops, places)
            rows = pl.ds(pl.multiple_of(place * share + first_row, HEAD_SIZE), refs[i].shape[1])
            term = lax.dot_general(refs[i][...], weight_ref[rows, here], PLAIN, preferred_element_type=jnp.float32)
            total = term if total is None else total + term
        if last:
            tile_ref, sems = refs[-2], refs[-1]
            tile_ref[step] = total.astype(out_ref.dtype)
            copies.append(pltpu.make_async_copy(tile_ref.at[step], out_ref.at[:, here], sems.at[step]))
            copies[-1].start()
        else:
            out_ref[:, here] = total
    for copy in copies:
        copy.wait()


def project(pieces, starts, weight, total, name, last=False, columns=512, flops=2**20):
    rows, width = pieces[0].shape[0], weight.shape[1]
    carried = total is not None
    args = [*pieces, weight] + [total] * carried
    tiles = width // columns
    if last:
        rest = dict(
            out_specs=pl.BlockSpec(memory_space=pl.ANY),
            scratch_shapes=[pltpu.VMEM((tiles, rows, columns), jnp.bfloat16), pltpu.SemaphoreType.DMA((tiles,))],
        )
    else:
        rest = dict(out_specs=VMEM, input_output_aliases={len(args) - 1: 0} if carried else {})
    return pl.pallas_call(
        functools.partial(project_kernel, len(pieces), carried, last, columns, starts),
        in_specs=[VMEM] * len(args),
        out_shape=jax.ShapeDtypeStruct((rows, width), jnp.bfloat16 if last else jnp.float32),
        compiler_params=pltpu.CompilerParams(vmem_limit_bytes=6 * 2**20),
        cost_estimate=pl.CostEstimate(flops=flops, bytes_accessed=2**10, transcendentals=0),
        name=name,
        **rest,
    )(*args)


def once_here(value, *others):
    anywhere = pl.BlockSpec(memory_space=pl.ANY)
    return pl.pallas_call(
        lambda *refs: None,
        in_specs=[anywhere] * (1 + len(others)),
        out_specs=anywhere,
        out_shape=jax.ShapeDtypeStruct(value.shape, value.dtype),
        input_output_aliases={0: 0},
        compiler_params=pltpu.CompilerParams(vmem_limit_bytes=2**20),
        cost_estimate=pl.CostEstimate(flops=0, bytes_accessed=0, transcendentals=0),
        name="once_here",
    )(value, *others)


def shards(queries, keys, values, doc_ids, out_weight):
    rows = keys.shape[0]
    shard = lax.axis_index("ctx")
    shard_count = lax.axis_size("ctx")
    places = lax.axis_size("head")
    other_core = [(i, i ^ 1) for i in range(shard_count)]

    def along_ctx(block, pairs):
        return lax.ppermute(block, "ctx", pairs)

    def along_head(block, step):
        return lax.ppermute(block, "head", [(i, (i + step) % places) for i in range(places)])

    own = jnp.concatenate([keys, values], 0)
    two_behind = along_ctx(own, [(i, i + 2) for i in range(shard_count - 2)])
    three_behind = along_ctx(own, [(i, i + 3) for i in range(1, shard_count - 3, 2)])
    window = (REACH + 1) * rows
    padded = jnp.concatenate([jnp.full((REACH * rows,), -1, jnp.int32), doc_ids], 0)
    kdoc = lax.dynamic_slice_in_dim(padded, shard * rows, window, 0)
    kdoc = kdoc[None, :]

    split = 5
    *state, qdoc, own_again = attend_own(queries, own, kdoc, split)
    beside = along_ctx(own_again, other_core)
    two_behind = once_here(two_behind, state[0])
    beside_two = along_ctx(two_behind, other_core)
    first_state = attend_two_behind(queries, two_behind, qdoc, kdoc, state)
    three_behind = once_here(three_behind, beside, beside_two, first_state[0])
    parts = (beside, two_behind, beside_two, three_behind)
    a = attend_rest(queries, parts, qdoc, kdoc, first_state)
    a_up = along_head(a, 1)
    a_down = along_head(a, -1)
    b, held = attend_whole(queries, parts, qdoc, kdoc, own, split, out_weight)
    b_up = along_head(b, 1)
    b_down = along_head(b, -1)
    b_row = split * HEAD_SIZE
    up, down, across = places - 1, 1, places // 2
    total = project([a, b], [(0, 0), (0, b_row)], held, None, "project_own")
    a_up = once_here(a_up, total)
    a_far = along_head(a_up, 1)
    total = project([a_up, a_down], [(up, 0), (down, 0)], held, total, "project_a")
    b_down = once_here(b_down, b_up, total)
    b_far = along_head(b_down, -1)
    total = project([b_up, b_down], [(up, b_row), (down, b_row)], held, total, "project_b")
    total = project([b_far], [(across, b_row)], held, total, "project_b_far")
    return project([a_far], [(across, 0)], held, total, "project_a_far", last=True)


def solution(mesh):
    in_specs = (P("ctx", "head"), P("ctx", "head"), P("ctx", "head"), P(), P(None, "head"))
    out_specs = P("ctx", "head")
    return jax.shard_map(shards, mesh=mesh, in_specs=in_specs, out_specs=out_specs, check_vma=False)
```
